512 devices in a mesh: member: 16 (over y, z_hi), dp: 32 (over x, z_lo, core).
Axes of the slice: x: 4, y: 4, z: 16 (z_hi: 4, z_lo: 4; z = z_hi * 4 + z_lo), core: 2. Of those that a mesh axis runs over, the one named last changes fastest.
Arguments:
- features: bfloat16 [16, 512, 49, 1024], P('member', 'dp'), may hold values from -8 to 8
- labels: int32 [512], replicated, may hold values from 0 to 24575
- norm_gain: float32 [16, 1024], P('member'), may hold values from 0.75 to 1.25
- norm_bias: float32 [16, 1024], P('member'), may hold values from -0.25 to 0.25
- head_weight: bfloat16 [16, 1024, 24576], P('member', None, 'dp'), may hold values from -3 to 3
- head_bias: float32 [16, 24576], P('member', 'dp'), may hold values from -1.25 to 1.25
Outputs:
- mean_loss: float32 [], replicated
- grad_pooled: float32 [16, 512, 1024], P('member', 'dp')
- grad_gain: float32 [16, 1024], P('member')
- grad_bias: float32 [16, 1024], P('member')
- grad_head_weight: bfloat16 [16, 1024, 24576], P('member', None, 'dp')
- grad_head_bias: float32 [16, 24576], P('member', 'dp')
The draws below stay inside these ranges and needn't reach their ends.
All inputs are finite; a program needn't handle non-finite values.
Results may differ from the reference program's by a relative error of at most 0.025.
Values may be sent and summed in bfloat16 or wider, within the bound.
No kernel may reach another device: no remote copies, remote signals or barrier semaphores. Data moves between devices by JAX's collectives and lax.ppermute only.
A program may use at most 64 MiB of HBM per device.

```python
import math
import jax
import jax.numpy as jnp
from jax import lax

C = 1024
POS = 49
IMAGES = 512
CLASSES = 24576
MEMBERS = 16


def draw_head_weight(key, part):
    column_scale = 3.2 / math.sqrt(C)
    shared = jnp.clip(jax.random.normal(jax.random.fold_in(key, 101), (1, C, CLASSES), jnp.float32), -6.0, 6.0)
    own = jnp.clip(jax.random.normal(jax.random.fold_in(key, 107), (MEMBERS, C, CLASSES), jnp.float32), -6.0, 6.0)
    common_dir = jnp.clip(jax.random.normal(jax.random.fold_in(key, 108), (MEMBERS, C, 1), jnp.float32), -4.0, 4.0)
    weight = (0.9968 * shared + 0.08 * own) * column_scale + 0.15 * common_dir
    return weight.astype(jnp.bfloat16)


def draw_features(key, part):
    full_shape = (MEMBERS, IMAGES, POS, C)
    shared_shape = (1, IMAGES, POS, C)
    shared = jax.random.normal(jax.random.fold_in(key, 102), shared_shape, jnp.float32)
    own = jax.random.normal(jax.random.fold_in(key, 109), full_shape, jnp.float32)
    values = 0.9968 * shared + 0.08 * own
    return jnp.clip(values, -8.0, 8.0).astype(jnp.bfloat16)


def touch_ends(result, rng, least, largest):
    spot = [jax.random.randint(jax.random.fold_in(rng, axis), (), 0, length) for axis, length in enumerate(result.shape)]
    widest = result.shape.index(max(result.shape))
    beside = spot[:widest] + [(spot[widest] + 1) % result.shape[widest]] + spot[widest + 1:]
    return result.at[tuple(spot)].set(least).at[tuple(beside)].set(largest)


def shard_levels(key, shape, pieces, smallest, top_value):
    gain, own = 1.0, jax.random.fold_in(key, 6)
    for dim, blocks in pieces:
        steps = jnp.exp(jax.random.uniform(jax.random.fold_in(own, dim), (blocks,), jnp.float32, smallest / len(pieces), top_value / len(pieces)))
        gain = gain * jnp.repeat(steps, shape[dim] // blocks).reshape([-1 if axis == dim else 1 for axis in range(len(shape))])
    return gain


def scatter_about(key, extent, deviation, reach, cuts=(), kind=jnp.bfloat16):
    array = deviation * jax.random.normal(key, extent, jnp.float32)
    if cuts:
        array = array * shard_levels(key, extent, cuts, -0.22, 0.18)
    return jnp.clip(array, -reach, reach).astype(kind)


def setup_inputs(seed: int = 0) -> dict:
    seeds = jax.random.split(jax.random.key(seed), 7)
    return {
        "features": draw_features(jax.random.fold_in(seeds[6], 71), 0),
        "labels": touch_ends(jax.random.randint(seeds[1], (IMAGES,), 0, CLASSES), jax.random.fold_in(seeds[1], 1), 0, CLASSES - 1).astype(jnp.int32),
        "norm_gain": jnp.clip(1.0 + 0.05 * jax.random.normal(seeds[2], (MEMBERS, C), jnp.float32), 0.75, 1.25),
        "norm_bias": scatter_about(seeds[3], (MEMBERS, C), 0.05, 0.25, ((0, 16),), jnp.float32),
        "head_weight": draw_head_weight(jax.random.fold_in(seeds[6], 71), 0),
        "head_bias": scatter_about(seeds[5], (MEMBERS, CLASSES), 0.25, 1.25, ((0, 16), (1, 32)), jnp.float32),
    }


norm_eps = 1e-06
loss_scale = 16.0

def layer_norm(pooled, norm_gain, norm_shift):
    center = pooled - lax.optimization_barrier(jnp.mean(pooled, axis=-1, keepdims=True))
    inverse = lax.rsqrt(lax.optimization_barrier(jnp.mean(center * center, axis=-1, keepdims=True)) + norm_eps)
    normed = center * inverse
    return (normed, inverse, (normed * norm_gain + norm_shift).astype(jnp.bfloat16))

def norm_backward(upstream, normed, inverse, norm_gain):
    scaled = upstream * norm_gain
    return inverse * (scaled - lax.optimization_barrier(jnp.mean(scaled, axis=-1, keepdims=True)) - normed * lax.optimization_barrier(jnp.mean(scaled * normed, axis=-1, keepdims=True)))

def member_forward(feature, gain_row, shift_row, weight, bias_row):
    pooled = lax.optimization_barrier(jnp.sum(feature, axis=1, dtype=jnp.float32)) / POS
    normed, inverse, act = layer_norm(pooled, gain_row, shift_row)
    logits = jnp.dot(act, weight, preferred_element_type=jnp.float32) + bias_row
    return (normed, inverse, act, logits)

def reference(features, labels, norm_gain, norm_bias, head_weight, head_bias):
    onehot = (labels[:, None] == jnp.arange(CLASSES, dtype=jnp.int32)[None, :]).astype(jnp.float32)

    def first_pass(items):
        normed, inverse, act, logits = member_forward(*items)
        highest = lax.optimization_barrier(jnp.max(logits, axis=1))
        log_total = highest + jnp.log(lax.optimization_barrier(jnp.sum(jnp.exp(logits - highest[:, None]), axis=1)))
        label_logit = lax.optimization_barrier(jnp.sum(logits * onehot, axis=1))
        return (label_logit - log_total, log_total)
    label_logp, log_totals = lax.map(first_pass, (features, norm_gain, norm_bias, head_weight, head_bias))
    highest = lax.optimization_barrier(jnp.max(label_logp, axis=0))
    log_joint = highest + jnp.log(lax.optimization_barrier(jnp.sum(jnp.exp(label_logp - highest[None, :]), axis=0)))
    mean_loss = math.log(MEMBERS) - jnp.mean(log_joint)
    respons = jnp.exp(label_logp - log_joint[None, :])

    def second_pass(items):
        feature, gain_row, shift_row, weight, bias_row, resp_row, total_row = items
        normed, inverse, act, logits = member_forward(feature, gain_row, shift_row, weight, bias_row)
        probabilities = jnp.exp(logits - total_row[:, None])
        grad_logits = (loss_scale * resp_row)[:, None] * (probabilities - onehot)
        grad_low = grad_logits.astype(jnp.bfloat16)
        grad_head_bias = lax.optimization_barrier(jnp.sum(grad_logits, axis=0))
        grad_head_weight = jnp.dot(act.T, grad_low, preferred_element_type=jnp.float32).astype(jnp.bfloat16)
        upstream = jnp.dot(grad_low, weight.T, preferred_element_type=jnp.float32)
        grad_gain = lax.optimization_barrier(jnp.sum(upstream * normed, axis=0))
        grad_shift = lax.optimization_barrier(jnp.sum(upstream, axis=0))
        grad_pooled = norm_backward(upstream, normed, inverse, gain_row)
        return (grad_pooled, grad_gain, grad_shift, grad_head_weight, grad_head_bias)
    grad_pooled, grad_gain, grad_bias, grad_head_weight, grad_head_bias = lax.map(second_pass, (features, norm_gain, norm_bias, head_weight, head_bias, respons, log_totals))
    return (mean_loss, grad_pooled, grad_gain, grad_bias, grad_head_weight, grad_head_bias)
```

```python
import math

import jax
import jax.numpy as jnp
from jax import lax
from jax.sharding import PartitionSpec as P

norm_eps = 1e-06
loss_scale = 16.0


def layer_norm(pooled, norm_gain, norm_shift):
    center = pooled - jnp.mean(pooled, axis=-1, keepdims=True)
    inverse = lax.rsqrt(jnp.mean(center * center, axis=-1, keepdims=True) + norm_eps)
    normed = center * inverse
    return (normed, inverse, (normed * norm_gain + norm_shift).astype(jnp.bfloat16))


def norm_backward(upstream, normed, inverse, norm_gain):
    scaled = upstream * norm_gain
    return inverse * (
        scaled
        - jnp.mean(scaled, axis=-1, keepdims=True)
        - normed * jnp.mean(scaled * normed, axis=-1, keepdims=True)
    )


def per_device(features, labels, norm_gain, norm_bias, head_weight, head_bias):
    dp = lax.axis_size("dp")
    members = lax.axis_size("member")
    chips = dp // 2
    position = lax.axis_index("dp")
    core = lax.rem(position, 2)
    swap = [(i, i ^ 1) for i in range(dp)]
    planes = [[2 * chip + c for chip in range(chips)] for c in range(2)]

    def over_plane(x):
        return lax.all_to_all(x, "dp", 0, 0, axis_index_groups=planes)

    weight = head_weight[0]
    classes_here = weight.shape[1]
    gain_row = norm_gain[0]
    shift_row = norm_bias[0]
    images_here = features.shape[1]
    plane_images = chips * images_here

    weight_other = lax.ppermute(weight, "dp", swap)
    bias_other = lax.ppermute(head_bias[0], "dp", swap)

    pooled = jnp.sum(features[0], axis=1, dtype=jnp.float32) / features.shape[2]
    normed, inverse, act = layer_norm(pooled, gain_row, shift_row)
    act_plane = over_plane(jnp.broadcast_to(act[None], (chips,) + act.shape)).reshape(
        plane_images, -1
    )
    act_other = lax.ppermute(act_plane, "dp", swap)

    plane_labels = lax.dynamic_index_in_dim(
        labels.reshape(chips, 2, images_here), core, axis=1, keepdims=False
    ).reshape(plane_images)
    class_ids = jnp.arange(classes_here, dtype=jnp.int32)[None, :]
    onehot_mine = (plane_labels - position * classes_here)[:, None] == class_ids
    onehot_other = (plane_labels - (position ^ 1) * classes_here)[:, None] == class_ids
    logits_mine = jnp.dot(act_plane, weight, preferred_element_type=jnp.float32) + head_bias[0]
    logits_other = (
        jnp.dot(act_plane, weight_other, preferred_element_type=jnp.float32) + bias_other
    )
    top = jnp.maximum(jnp.max(logits_mine, axis=1), jnp.max(logits_other, axis=1))
    total = jnp.sum(jnp.exp(logits_mine - top[:, None]), axis=1) + jnp.sum(
        jnp.exp(logits_other - top[:, None]), axis=1
    )
    label_part = jnp.sum(jnp.where(onehot_mine, logits_mine, 0.0), axis=1) + jnp.sum(
        jnp.where(onehot_other, logits_other, 0.0), axis=1
    )
    stats = jnp.stack([top + jnp.log(total), label_part])
    stats_all = over_plane(jnp.broadcast_to(stats[None], (chips,) + stats.shape))
    logs = stats_all[:, 0]
    logs_top = jnp.max(logs, axis=0)
    log_total = logs_top + jnp.log(jnp.sum(jnp.exp(logs - logs_top), axis=0))
    label_logp = jnp.sum(stats_all[:, 1], axis=0) - log_total

    logp_all = lax.all_to_all(
        jnp.broadcast_to(label_logp[None], (members, plane_images)), "member", 0, 0
    )

    diff_mine = jnp.exp(logits_mine - log_total[:, None]) - onehot_mine.astype(jnp.float32)
    diff_other = jnp.exp(logits_other - log_total[:, None]) - onehot_other.astype(jnp.float32)
    low_mine = diff_mine.astype(jnp.bfloat16)
    low_other = diff_other.astype(jnp.bfloat16)
    contract = (((1,), (1,)), ((), ()))
    partial = lax.dot_general(
        low_mine, weight, contract, preferred_element_type=jnp.float32
    ) + lax.dot_general(low_other, weight_other, contract, preferred_element_type=jnp.float32)
    pieces = over_plane(partial.astype(jnp.bfloat16).reshape(chips, images_here, -1))
    low_received = lax.ppermute(low_other, "dp", swap)

    joint_top = jnp.max(logp_all, axis=0)
    log_joint = joint_top + jnp.log(jnp.sum(jnp.exp(logp_all - joint_top), axis=0))
    scale = loss_scale * jnp.exp(label_logp - log_joint)

    shift_sum = jnp.sum(scale[:, None] * partial, axis=0)
    act_sum = jnp.sum(scale[:, None] * partial * act_plane.astype(jnp.float32), axis=0)
    sums = jnp.stack([shift_sum, act_sum])
    sums = jnp.sum(
        lax.all_to_all(jnp.broadcast_to(sums[None], (dp,) + sums.shape), "dp", 0, 0), axis=0
    )
    grad_shift = sums[0]
    grad_gain = (sums[1] - shift_row * grad_shift) / gain_row

    grad_other = jnp.sum(scale[:, None] * diff_other, axis=0)
    note = jnp.concatenate([scale, log_joint, grad_other])
    note = lax.ppermute(note, "dp", swap)
    scale_other = note[:plane_images]
    mean_loss = math.log(members) - (
        jnp.sum(log_joint) + jnp.sum(note[plane_images : 2 * plane_images])
    ) / (2 * plane_images)
    grad_mine = scale[:, None] * diff_mine
    grad_head_bias = jnp.sum(grad_mine, axis=0) + note[2 * plane_images :]
    rows = (((0,), (0,)), ((), ()))
    grad_head_weight = (
        lax.dot_general(
            act_plane, grad_mine.astype(jnp.bfloat16), rows, preferred_element_type=jnp.float32
        )
        + lax.dot_general(
            act_other,
            (scale_other[:, None] * low_received.astype(jnp.float32)).astype(jnp.bfloat16),
            rows,
            preferred_element_type=jnp.float32,
        )
    ).astype(jnp.bfloat16)

    scale_own = lax.dynamic_slice_in_dim(scale, (position // 2) * images_here, images_here)
    upstream = scale_own[:, None] * jnp.sum(pieces.astype(jnp.float32), axis=0)
    grad_pooled = norm_backward(upstream, normed, inverse, gain_row)
    return (
        mean_loss,
        grad_pooled[None],
        grad_gain[None],
        grad_shift[None],
        grad_head_weight[None],
        grad_head_bias[None],
    )


def solution(mesh):
    in_specs = (
        P("member", "dp", None, None),
        P(),
        P("member", None),
        P("member", None),
        P("member", None, "dp"),
        P("member", "dp"),
    )
    out_specs = (
        P(),
        P("member", "dp", None),
        P("member", None),
        P("member", None),
        P("member", None, "dp"),
        P("member", "dp"),
    )
    return jax.shard_map(
        per_device, mesh=mesh, in_specs=in_specs, out_specs=out_specs, check_vma=False
    )
```

```python
import math

import jax
import jax.numpy as jnp
from jax import lax
from jax.sharding import PartitionSpec as P

norm_eps = 1e-06
loss_scale = 16.0


def layer_norm(pooled, norm_gain, norm_shift):
    center = pooled - jnp.mean(pooled, axis=-1, keepdims=True)
    inverse = lax.rsqrt(jnp.mean(center * center, axis=-1, keepdims=True) + norm_eps)
    normed = center * inverse
    return (normed, inverse, (normed * norm_gain + norm_shift).astype(jnp.bfloat16))


def norm_backward(upstream, normed, inverse, norm_gain):
    scaled = upstream * norm_gain
    return inverse * (
        scaled
        - jnp.mean(scaled, axis=-1, keepdims=True)
        - normed * jnp.mean(scaled * normed, axis=-1, keepdims=True)
    )


def per_device(features, labels, norm_gain, norm_bias, head_weight, head_bias):
    dp = lax.axis_size("dp")
    members = lax.axis_size("member")
    chips = dp // 2
    position = lax.axis_index("dp")
    core = lax.rem(position, 2)
    swap = [(i, i ^ 1) for i in range(dp)]
    planes = [[2 * chip + c for chip in range(chips)] for c in range(2)]

    def over_plane(x):
        return lax.all_to_all(x, "dp", 0, 0, axis_index_groups=planes)

    weight = head_weight[0]
    classes_here = weight.shape[1]
    gain_row = norm_gain[0]
    shift_row = norm_bias[0]
    images_here = features.shape[1]
    plane_images = chips * images_here

    weight_other = lax.ppermute(weight, "dp", swap)
    bias_other = lax.ppermute(head_bias[0], "dp", swap)

    pooled = jnp.sum(features[0], axis=1, dtype=jnp.float32) / features.shape[2]
    normed, inverse, act = layer_norm(pooled, gain_row, shift_row)
    act_plane = over_plane(jnp.broadcast_to(act[None], (chips,) + act.shape)).reshape(
        plane_images, -1
    )
    act_other = lax.ppermute(act_plane, "dp", swap)

    plane_labels = lax.dynamic_index_in_dim(
        labels.reshape(chips, 2, images_here), core, axis=1, keepdims=False
    ).reshape(plane_images)
    class_ids = jnp.arange(classes_here, dtype=jnp.int32)
    both_ids = jnp.concatenate(
        [position * classes_here + class_ids, (position ^ 1) * classes_here + class_ids]
    )
    weight_both = jnp.concatenate([weight, weight_other], axis=1)
    bias_both = jnp.concatenate([head_bias[0], bias_other])
    onehot = plane_labels[:, None] == both_ids[None, :]
    logits = jnp.dot(act_plane, weight_both, preferred_element_type=jnp.float32) + bias_both
    top = jnp.max(logits, axis=1)
    total = jnp.sum(jnp.exp(logits - top[:, None]), axis=1)
    label_part = jnp.sum(jnp.where(onehot, logits, 0.0), axis=1)
    stats = jnp.stack([top + jnp.log(total), label_part])
    stats_all = over_plane(jnp.broadcast_to(stats[None], (chips,) + stats.shape))
    logs = stats_all[:, 0]
    logs_top = jnp.max(logs, axis=0)
    log_total = logs_top + jnp.log(jnp.sum(jnp.exp(logs - logs_top), axis=0))
    label_logp = jnp.sum(stats_all[:, 1], axis=0) - log_total

    logp_all = lax.all_to_all(
        jnp.broadcast_to(label_logp[None], (members, plane_images)), "member", 0, 0
    )

    diff = jnp.exp(logits - log_total[:, None]) - onehot.astype(jnp.float32)
    low = diff.astype(jnp.bfloat16)
    partial = lax.dot_general(
        low, weight_both, (((1,), (1,)), ((), ())), preferred_element_type=jnp.float32
    )
    low_received = lax.ppermute(low[:, classes_here:], "dp", swap)

    joint_top = jnp.max(logp_all, axis=0)
    log_joint = joint_top + jnp.log(jnp.sum(jnp.exp(logp_all - joint_top), axis=0))
    scale = loss_scale * jnp.exp(label_logp - log_joint)

    shift_sum = jnp.sum(scale[:, None] * partial, axis=0)
    act_sum = jnp.sum(scale[:, None] * (partial * act_plane.astype(jnp.float32)), axis=0)
    sums = jnp.stack([shift_sum, act_sum])
    sums_high = sums.astype(jnp.bfloat16)
    sums_low = (sums - sums_high.astype(jnp.float32)).astype(jnp.bfloat16)
    tail = jnp.concatenate([sums_high, sums_low]).reshape(images_here, -1)
    chunks = jnp.concatenate(
        [
            partial.astype(jnp.bfloat16).reshape(chips, images_here, -1),
            jnp.broadcast_to(tail[None], (chips,) + tail.shape),
        ],
        axis=2,
    )
    pieces = over_plane(chunks)
    channels = act.shape[1]
    received = jnp.sum(pieces.astype(jnp.float32), axis=0)
    sums = received[:, channels:].reshape(2, 2, channels)
    sums = sums[0] + sums[1]
    sums = sums + lax.ppermute(sums, "dp", swap)
    grad_shift = sums[0]
    grad_gain = (sums[1] - shift_row * grad_shift) / gain_row

    grad_logits = scale[:, None] * diff
    grad_sum = jnp.sum(grad_logits, axis=0)
    note = jnp.concatenate([scale, log_joint, grad_sum[classes_here:]])
    note = lax.ppermute(note, "dp", swap)
    scale_other = note[:plane_images]
    mean_loss = math.log(members) - (
        jnp.sum(log_joint) + jnp.sum(note[plane_images : 2 * plane_images])
    ) / (2 * plane_images)
    grad_head_bias = grad_sum[:classes_here] + note[2 * plane_images :]
    rows = (((0,), (0,)), ((), ()))
    grad_head_weight = (
        lax.dot_general(
            act_plane,
            grad_logits[:, :classes_here].astype(jnp.bfloat16),
            rows,
            preferred_element_type=jnp.float32,
        )
        + lax.dot_general(
            act_other,
            (scale_other[:, None] * low_received.astype(jnp.float32)).astype(jnp.bfloat16),
            rows,
            preferred_element_type=jnp.float32,
        )
    ).astype(jnp.bfloat16)

    scale_own = lax.dynamic_slice_in_dim(scale, (position // 2) * images_here, images_here)
    upstream = scale_own[:, None] * received[:, :channels]
    grad_pooled = norm_backward(upstream, normed, inverse, gain_row)
    return (
        mean_loss,
        grad_pooled[None],
        grad_gain[None],
        grad_shift[None],
        grad_head_weight[None],
        grad_head_bias[None],
    )


def solution(mesh):
    in_specs = (
        P("member", "dp", None, None),
        P(),
        P("member", None),
        P("member", None),
        P("member", None, "dp"),
        P("member", "dp"),
    )
    out_specs = (
        P(),
        P("member", "dp", None),
        P("member", None),
        P("member", None),
        P("member", None, "dp"),
        P("member", "dp"),
    )
    return jax.shard_map(
        per_device, mesh=mesh, in_specs=in_specs, out_specs=out_specs, check_vma=False
    )
```

```python
import functools
import math

import jax
import jax.numpy as jnp
from jax import lax
from jax.experimental import pallas as pl
from jax.experimental.pallas import tpu as pltpu
from jax.sharding import PartitionSpec as P

norm_eps = 1e-06
loss_scale = 16.0


def norm_kernel(positions, total_ref, gain_ref, shift_ref, normed_ref, inverse_ref, act_ref):
    pooled = total_ref[...] / positions
    center = pooled - jnp.mean(pooled, axis=-1, keepdims=True)
    inverse = lax.rsqrt(jnp.mean(center * center, axis=-1, keepdims=True) + norm_eps)
    normed = center * inverse
    normed_ref[...] = normed
    inverse_ref[...] = jnp.broadcast_to(inverse, inverse_ref.shape)
    act = (normed * gain_ref[...] + shift_ref[...]).astype(jnp.bfloat16)
    act_ref[...] = jnp.broadcast_to(act[None], act_ref.shape)


def norm_copies(total, positions, gain_row, shift_row, copies):
    images, channels = total.shape
    whole = lambda *shape: pl.BlockSpec(shape, lambda i: (0,) * len(shape))
    return pl.pallas_call(
        functools.partial(norm_kernel, positions),
        grid=(1,),
        in_specs=[whole(images, channels), whole(1, channels), whole(1, channels)],
        out_specs=[
            whole(images, channels),
            whole(images, 128),
            whole(copies, images, channels),
        ],
        out_shape=[
            jax.ShapeDtypeStruct((images, channels), jnp.float32),
            jax.ShapeDtypeStruct((images, 128), jnp.float32),
            jax.ShapeDtypeStruct((copies, images, channels), jnp.bfloat16),
        ],
        compiler_params=pltpu.CompilerParams(vmem_limit_bytes=16 * 2**20),
    )(total, gain_row, shift_row)


def join_kernel(logp_ref, own_ref, partial_ref, act_ref, _, scale_ref, joint_ref, tail_ref):
    logp = logp_ref[...]
    top = jnp.max(logp, axis=0, keepdims=True)
    joint = top + jnp.log(jnp.sum(jnp.exp(logp - top), axis=0, keepdims=True))
    joint_ref[...] = joint
    scale = loss_scale * jnp.exp(own_ref[...] - joint)
    images = scale.shape[1]
    column = jnp.transpose(jnp.broadcast_to(scale, (128, images)))
    scale_ref[...] = column
    scaled = partial_ref[...] * column[:, :1]
    sums = [
        jnp.sum(scaled, axis=0, keepdims=True),
        jnp.sum(scaled * act_ref[...].astype(jnp.float32), axis=0, keepdims=True),
    ]
    high = [x.astype(jnp.bfloat16).astype(jnp.float32) for x in sums]
    low = [x - h for x, h in zip(sums, high)]
    width = tail_ref.shape[2]
    lines = [x[:, k : k + width] for x in high + low for k in range(0, x.shape[1], width)]
    tail = jnp.concatenate(lines, axis=0).astype(jnp.bfloat16)
    tail_ref[...] = jnp.broadcast_to(tail[None], tail_ref.shape)


def join_members(logp_all, label_logp, partial, act, chunks):
    images, channels = act.shape
    width = chunks.shape[2] - channels
    whole = lambda *shape: pl.BlockSpec(shape, lambda i: (0,) * len(shape))
    return pl.pallas_call(
        join_kernel,
        grid=(1,),
        in_specs=[
            whole(*logp_all.shape),
            whole(1, images),
            whole(images, channels),
            whole(images, channels),
            pl.BlockSpec(memory_space=pl.ANY),
        ],
        out_specs=[
            whole(images, 128),
            whole(1, images),
            pl.BlockSpec(chunks.shape[:2] + (width,), lambda i: (0, 0, channels // width)),
        ],
        out_shape=[
            jax.ShapeDtypeStruct((images, 128), jnp.float32),
            jax.ShapeDtypeStruct((1, images), jnp.float32),
            jax.ShapeDtypeStruct(chunks.shape, chunks.dtype),
        ],
        input_output_aliases={4: 2},
        compiler_params=pltpu.CompilerParams(vmem_limit_bytes=24 * 2**20),
    )(logp_all, label_logp, partial, act, chunks)


def close_kernel(_, pieces_ref, scale_ref, normed_ref, inverse_ref, gain_ref, grad_ref):
    received = pieces_ref[0].astype(jnp.float32)
    for k in range(1, pieces_ref.shape[0]):
        received = received + pieces_ref[k].astype(jnp.float32)
    normed = normed_ref[...]
    scaled = scale_ref[:, :1] * received * gain_ref[...]
    grad_ref[...] = inverse_ref[:, :1] * (
        scaled
        - jnp.mean(scaled, axis=-1, keepdims=True)
        - normed * jnp.mean(scaled * normed, axis=-1, keepdims=True)
    )


def close_images(chip, pieces, scale, normed, inverse, gain_row):
    images, channels = normed.shape
    whole = lambda *shape: pl.BlockSpec(shape, lambda i, chip: (0,) * len(shape))
    return pl.pallas_call(
        close_kernel,
        grid_spec=pltpu.PrefetchScalarGridSpec(
            num_scalar_prefetch=1,
            grid=(1,),
            in_specs=[
                whole(pieces.shape[0], images, channels),
                pl.BlockSpec((images, 128), lambda i, chip: (chip[0], 0)),
                whole(images, channels),
                whole(images, 128),
                whole(1, channels),
            ],
            out_specs=whole(images, channels),
        ),
        out_shape=jax.ShapeDtypeStruct((images, channels), jnp.float32),
        cost_estimate=pl.CostEstimate(
            flops=40 * images * channels, bytes_accessed=2**20, transcendentals=0
        ),
        compiler_params=pltpu.CompilerParams(vmem_limit_bytes=16 * 2**20),
    )(jnp.reshape(chip, (1,)), pieces, scale, normed, inverse, gain_row)


def sum_tails_kernel(tails_ref, sums_ref):
    tail = tails_ref[0].astype(jnp.float32)
    for k in range(1, tails_ref.shape[0]):
        tail = tail + tails_ref[k].astype(jnp.float32)
    lines, width = tail.shape
    half, quarter = lines // 2, lines // 4
    tail = tail[:half] + tail[half:]
    for r in range(2):
        for k in range(quarter):
            sums_ref[r : r + 1, k * width : (k + 1) * width] = tail[r * quarter + k][None]


def sum_tails(pieces, channels):
    copies, lines, whole_width = pieces.shape
    width = whole_width - channels
    return pl.pallas_call(
        sum_tails_kernel,
        grid=(1,),
        in_specs=[pl.BlockSpec((copies, lines, width), lambda i: (0, 0, channels // width))],
        out_specs=pl.BlockSpec((2, channels), lambda i: (0, 0)),
        out_shape=jax.ShapeDtypeStruct((2, channels), jnp.float32),
        compiler_params=pltpu.CompilerParams(vmem_limit_bytes=16 * 2**20),
    )(pieces)


def per_device(features, labels, norm_gain, norm_bias, head_weight, head_bias):
    dp = lax.axis_size("dp")
    members = lax.axis_size("member")
    chips = dp // 2
    position = lax.axis_index("dp")
    core = lax.rem(position, 2)
    swap = [(i, i ^ 1) for i in range(dp)]
    planes = [[2 * chip + c for chip in range(chips)] for c in range(2)]

    def over_plane(x):
        return lax.all_to_all(x, "dp", 0, 0, axis_index_groups=planes)

    weight = head_weight[0]
    classes_here = weight.shape[1]
    gain_row = norm_gain[0]
    shift_row = norm_bias[0]
    images_here = features.shape[1]
    plane_images = chips * images_here

    weight_other = lax.ppermute(weight, "dp", swap)
    bias_other = lax.ppermute(head_bias[0], "dp", swap)

    normed, inverse, act_copies = norm_copies(
        jnp.sum(features[0], axis=1, dtype=jnp.float32),
        features.shape[2],
        norm_gain,
        norm_bias,
        chips,
    )
    channels = normed.shape[1]
    act_plane = over_plane(act_copies).reshape(plane_images, channels)

    plane_labels = lax.dynamic_index_in_dim(
        labels.reshape(chips, 2, images_here), core, axis=1, keepdims=False
    ).reshape(plane_images)
    class_ids = jnp.arange(classes_here, dtype=jnp.int32)
    both_ids = jnp.concatenate(
        [position * classes_here + class_ids, (position ^ 1) * classes_here + class_ids]
    )
    weight_both = jnp.concatenate([weight, weight_other], axis=1)
    bias_both = jnp.concatenate([head_bias[0], bias_other])
    onehot = plane_labels[:, None] == both_ids[None, :]
    logits = jnp.dot(act_plane, weight_both, preferred_element_type=jnp.float32) + bias_both
    top = jnp.max(logits, axis=1)
    total = jnp.sum(jnp.exp(logits - top[:, None]), axis=1)
    label_part = jnp.sum(jnp.where(onehot, logits, 0.0), axis=1)
    stats = jnp.stack([top + jnp.log(total), label_part])
    stats_all = over_plane(jnp.broadcast_to(stats[None], (chips,) + stats.shape))
    logs = stats_all[:, 0]
    logs_top = jnp.max(logs, axis=0)
    log_total = logs_top + jnp.log(jnp.sum(jnp.exp(logs - logs_top), axis=0))
    label_logp = jnp.sum(stats_all[:, 1], axis=0) - log_total

    logp_all = lax.all_to_all(
        jnp.broadcast_to(label_logp[None], (members, plane_images)), "member", 0, 0
    )

    diff = jnp.exp(logits - log_total[:, None]) - onehot.astype(jnp.float32)
    low = diff.astype(jnp.bfloat16)
    partial = lax.dot_general(
        low, weight_both, (((1,), (1,)), ((), ())), preferred_element_type=jnp.float32
    )
    tail_columns = 4 * channels // images_here
    chunks = jnp.pad(
        partial.astype(jnp.bfloat16).reshape(chips, images_here, channels),
        ((0, 0), (0, 0), (0, tail_columns)),
    )
    diff, partial, chunks = lax.optimization_barrier((diff, partial, chunks))
    scale, log_joint, chunks = join_members(
        logp_all, label_logp[None], partial, act_plane, chunks
    )
    pieces = over_plane(chunks)

    grad_logits = scale[:, :1] * diff
    grad_sum = jnp.sum(grad_logits, axis=0)
    note = jnp.concatenate([log_joint[0], grad_sum[classes_here:]])
    note = lax.ppermute(note, "dp", swap)
    mean_loss = math.log(members) - (
        jnp.sum(log_joint) + jnp.sum(note[:plane_images])
    ) / (2 * plane_images)
    grad_head_bias = grad_sum[:classes_here] + note[plane_images:]
    rows = (((0,), (0,)), ((), ()))
    grad_low = grad_logits.astype(jnp.bfloat16)
    for_other = lax.dot_general(
        act_plane, grad_low[:, classes_here:], rows, preferred_element_type=jnp.float32
    ).astype(jnp.bfloat16)
    from_other = lax.ppermute(for_other, "dp", swap)
    grad_head_weight = (
        lax.dot_general(
            act_plane, grad_low[:, :classes_here], rows, preferred_element_type=jnp.float32
        )
        + from_other.astype(jnp.float32)
    ).astype(jnp.bfloat16)

    pieces, grad_head_weight, grad_head_bias, mean_loss = lax.optimization_barrier(
        (pieces, grad_head_weight, grad_head_bias, mean_loss)
    )
    sums = sum_tails(pieces, channels)
    grad_pooled = close_images(position // 2, pieces, scale, normed, inverse, norm_gain)
    sums = sums + lax.ppermute(sums, "dp", swap)
    grad_shift = sums[0]
    grad_gain = (sums[1] - shift_row * grad_shift) / gain_row
    return (
        mean_loss,
        grad_pooled[None],
        grad_gain[None],
        grad_shift[None],
        grad_head_weight[None],
        grad_head_bias[None],
    )


def solution(mesh):
    in_specs = (
        P("member", "dp", None, None),
        P(),
        P("member", None),
        P("member", None),
        P("member", None, "dp"),
        P("member", "dp"),
    )
    out_specs = (
        P(),
        P("member", "dp", None),
        P("member", None),
        P("member", None),
        P("member", None, "dp"),
        P("member", "dp"),
    )
    return jax.shard_map(
        per_device, mesh=mesh, in_specs=in_specs, out_specs=out_specs, check_vma=False
    )
```

```python
import functools
import math

import jax
import jax.numpy as jnp
from jax import lax
from jax.experimental import pallas as pl
from jax.experimental.pallas import tpu as pltpu
from jax.sharding import PartitionSpec as P

norm_eps = 1e-06
loss_scale = 16.0


def norm_kernel(positions, total_ref, gain_ref, shift_ref, normed_ref, inverse_ref, act_ref):
    pooled = total_ref[...] / positions
    center = pooled - jnp.mean(pooled, axis=-1, keepdims=True)
    inverse = lax.rsqrt(jnp.mean(center * center, axis=-1, keepdims=True) + norm_eps)
    normed = center * inverse
    normed_ref[...] = normed
    inverse_ref[...] = jnp.broadcast_to(inverse, inverse_ref.shape)
    act = (normed * gain_ref[...] + shift_ref[...]).astype(jnp.bfloat16)
    act_ref[...] = jnp.broadcast_to(act[None], act_ref.shape)


def norm_copies(total, positions, gain_row, shift_row, copies):
    images, channels = total.shape
    whole = lambda *shape: pl.BlockSpec(shape, lambda i: (0,) * len(shape))
    return pl.pallas_call(
        functools.partial(norm_kernel, positions),
        grid=(1,),
        in_specs=[whole(images, channels), whole(1, channels), whole(1, channels)],
        out_specs=[
            whole(images, channels),
            whole(images, 128),
            whole(copies, images, channels),
        ],
        out_shape=[
            jax.ShapeDtypeStruct((images, channels), jnp.float32),
            jax.ShapeDtypeStruct((images, 128), jnp.float32),
            jax.ShapeDtypeStruct((copies, images, channels), jnp.bfloat16),
        ],
        compiler_params=pltpu.CompilerParams(vmem_limit_bytes=16 * 2**20),
    )(total, gain_row, shift_row)


def join_kernel(logp_ref, own_ref, partial_ref, act_ref, _, scale_ref, joint_ref, tail_ref):
    logp = logp_ref[...]
    top = jnp.max(logp, axis=0, keepdims=True)
    joint = top + jnp.log(jnp.sum(jnp.exp(logp - top), axis=0, keepdims=True))
    joint_ref[...] = joint
    scale = loss_scale * jnp.exp(own_ref[...] - joint)
    images = scale.shape[1]
    column = jnp.transpose(jnp.broadcast_to(scale, (128, images)))
    scale_ref[...] = column
    scaled = partial_ref[...] * column[:, :1]
    sums = [
        jnp.sum(scaled, axis=0, keepdims=True),
        jnp.sum(scaled * act_ref[...].astype(jnp.float32), axis=0, keepdims=True),
    ]
    high = [x.astype(jnp.bfloat16).astype(jnp.float32) for x in sums]
    low = [x - h for x, h in zip(sums, high)]
    width = tail_ref.shape[2]
    lines = [x[:, k : k + width] for x in high + low for k in range(0, x.shape[1], width)]
    tail = jnp.concatenate(lines, axis=0).astype(jnp.bfloat16)
    tail_ref[...] = jnp.broadcast_to(tail[None], tail_ref.shape)


def join_members(logp_all, label_logp, partial, act, chunks):
    images, channels = act.shape
    width = chunks.shape[2] - channels
    whole = lambda *shape: pl.BlockSpec(shape, lambda i: (0,) * len(shape))
    return pl.pallas_call(
        join_kernel,
        grid=(1,),
        in_specs=[
            whole(*logp_all.shape),
            whole(1, images),
            whole(images, channels),
            whole(images, channels),
            pl.BlockSpec(memory_space=pl.ANY),
        ],
        out_specs=[
            whole(images, 128),
            whole(1, images),
            pl.BlockSpec(chunks.shape[:2] + (width,), lambda i: (0, 0, channels // width)),
        ],
        out_shape=[
            jax.ShapeDtypeStruct((images, 128), jnp.float32),
            jax.ShapeDtypeStruct((1, images), jnp.float32),
            jax.ShapeDtypeStruct(chunks.shape, chunks.dtype),
        ],
        input_output_aliases={4: 2},
        compiler_params=pltpu.CompilerParams(vmem_limit_bytes=24 * 2**20),
    )(logp_all, label_logp, partial, act, chunks)


def close_kernel(
    place, pieces_ref, scale_ref, normed_ref, inverse_ref, gain_ref, shift_ref, sums_ref, bias_ref, *outs
):
    grad_ref, grad_gain_ref, grad_shift_ref, grad_bias_ref, joint_ref = outs
    received = pieces_ref[0].astype(jnp.float32)
    for k in range(1, pieces_ref.shape[0]):
        received = received + pieces_ref[k].astype(jnp.float32)
    normed = normed_ref[...]
    gain = gain_ref[...]
    scaled = scale_ref[:, :1] * received * gain
    grad_ref[...] = inverse_ref[:, :1] * (
        scaled
        - jnp.mean(scaled, axis=-1, keepdims=True)
        - normed * jnp.mean(scaled * normed, axis=-1, keepdims=True)
    )
    sums = sums_ref[0] + sums_ref[1]
    grad_shift_ref[...] = sums[:1]
    grad_gain_ref[...] = (sums[1:2] - shift_ref[...] * sums[:1]) / gain
    plane_images = sums.shape[1] - bias_ref.shape[1]
    other_note = jnp.where(place[1] == 0, sums_ref[1, 2:3], sums_ref[0, 2:3])
    grad_bias_ref[...] = bias_ref[...] + other_note[:, plane_images:]
    joint_ref[...] = jnp.mean(sums[2:3, :plane_images], axis=1, keepdims=True) / 2


def close_images(
    position, pieces, scale, normed, inverse, gain_row, shift_row, sums, bias_part
):
    images, channels = normed.shape
    whole = lambda *shape: pl.BlockSpec(shape, lambda i, place: (0,) * len(shape))
    small = [(1, channels), (1, channels), bias_part.shape, (1, 1)]
    return pl.pallas_call(
        close_kernel,
        grid_spec=pltpu.PrefetchScalarGridSpec(
            num_scalar_prefetch=1,
            grid=(1,),
            in_specs=[
                whole(pieces.shape[0], images, channels),
                pl.BlockSpec((images, 128), lambda i, place: (place[0], 0)),
                whole(images, channels),
                whole(images, 128),
                whole(1, channels),
                whole(1, channels),
                whole(*sums.shape),
                whole(*bias_part.shape),
            ],
            out_specs=[whole(images, channels)] + [whole(*shape) for shape in small],
        ),
        out_shape=[jax.ShapeDtypeStruct((images, channels), jnp.float32)]
        + [jax.ShapeDtypeStruct(shape, jnp.float32) for shape in small],
        compiler_params=pltpu.CompilerParams(vmem_limit_bytes=16 * 2**20),
    )(
        jnp.stack([position // 2, lax.rem(position, 2)]),
        pieces,
        scale,
        normed,
        inverse,
        gain_row,
        shift_row,
        sums,
        bias_part,
    )


def sum_tails_kernel(tails_ref, note_ref, sums_ref):
    tail = tails_ref[0].astype(jnp.float32)
    for k in range(1, tails_ref.shape[0]):
        tail = tail + tails_ref[k].astype(jnp.float32)
    lines, width = tail.shape
    half, quarter = lines // 2, lines // 4
    tail = tail[:half] + tail[half:]
    for r in range(2):
        for k in range(quarter):
            sums_ref[r : r + 1, k * width : (k + 1) * width] = tail[r * quarter + k][None]
    sums_ref[2:3] = note_ref[...]


def sum_tails(pieces, note):
    copies, lines, whole_width = pieces.shape
    channels = note.shape[1]
    width = whole_width - channels
    return pl.pallas_call(
        sum_tails_kernel,
        grid=(1,),
        in_specs=[
            pl.BlockSpec((copies, lines, width), lambda i: (0, 0, channels // width)),
            pl.BlockSpec((1, channels), lambda i: (0, 0)),
        ],
        out_specs=pl.BlockSpec((3, channels), lambda i: (0, 0)),
        out_shape=jax.ShapeDtypeStruct((3, channels), jnp.float32),
        compiler_params=pltpu.CompilerParams(vmem_limit_bytes=16 * 2**20),
    )(pieces, note)


def per_device(features, labels, norm_gain, norm_bias, head_weight, head_bias):
    dp = lax.axis_size("dp")
    members = lax.axis_size("member")
    chips = dp // 2
    position = lax.axis_index("dp")
    core = lax.rem(position, 2)
    swap = [(i, i ^ 1) for i in range(dp)]
    planes = [[2 * chip + c for chip in range(chips)] for c in range(2)]

    def over_plane(x):
        return lax.all_to_all(x, "dp", 0, 0, axis_index_groups=planes)

    weight = head_weight[0]
    classes_here = weight.shape[1]
    gain_row = norm_gain[0]
    shift_row = norm_bias[0]
    images_here = features.shape[1]
    plane_images = chips * images_here

    weight_other = lax.ppermute(weight, "dp", swap)
    bias_other = lax.ppermute(head_bias[0], "dp", swap)

    normed, inverse, act_copies = norm_copies(
        jnp.sum(features[0], axis=1, dtype=jnp.float32),
        features.shape[2],
        norm_gain,
        norm_bias,
        chips,
    )
    channels = normed.shape[1]
    act_plane = over_plane(act_copies).reshape(plane_images, channels)

    plane_labels = lax.dynamic_index_in_dim(
        labels.reshape(chips, 2, images_here), core, axis=1, keepdims=False
    ).reshape(plane_images)
    class_ids = jnp.arange(classes_here, dtype=jnp.int32)
    both_ids = jnp.concatenate(
        [position * classes_here + class_ids, (position ^ 1) * classes_here + class_ids]
    )
    weight_both = jnp.concatenate([weight, weight_other], axis=1)
    bias_both = jnp.concatenate([head_bias[0], bias_other])
    onehot = plane_labels[:, None] == both_ids[None, :]
    logits = jnp.dot(act_plane, weight_both, preferred_element_type=jnp.float32) + bias_both
    top = jnp.max(logits, axis=1)
    total = jnp.sum(jnp.exp(logits - top[:, None]), axis=1)
    label_part = jnp.sum(jnp.where(onehot, logits, 0.0), axis=1)
    stats = jnp.stack([top + jnp.log(total), label_part])
    stats_all = over_plane(jnp.broadcast_to(stats[None], (chips,) + stats.shape))
    logs = stats_all[:, 0]
    logs_top = jnp.max(logs, axis=0)
    log_total = logs_top + jnp.log(jnp.sum(jnp.exp(logs - logs_top), axis=0))
    label_logp = jnp.sum(stats_all[:, 1], axis=0) - log_total

    logp_all = lax.all_to_all(
        jnp.broadcast_to(label_logp[None], (members, plane_images)), "member", 0, 0
    )

    diff = jnp.exp(logits - log_total[:, None]) - onehot.astype(jnp.float32)
    low = diff.astype(jnp.bfloat16)
    partial = lax.dot_general(
        low, weight_both, (((1,), (1,)), ((), ())), preferred_element_type=jnp.float32
    )
    tail_columns = 4 * channels // images_here
    chunks = jnp.pad(
        partial.astype(jnp.bfloat16).reshape(chips, images_here, channels),
        ((0, 0), (0, 0), (0, tail_columns)),
    )
    diff, partial, chunks = lax.optimization_barrier((diff, partial, chunks))
    scale, log_joint, chunks = join_members(
        logp_all, label_logp[None], partial, act_plane, chunks
    )
    pieces = over_plane(chunks)

    rows = (((0,), (0,)), ((), ()))
    grad_other = scale[:, :1] * diff[:, classes_here:]
    bias_other_part = jnp.sum(grad_other, axis=0)
    for_other = lax.dot_general(
        act_plane, grad_other.astype(jnp.bfloat16), rows, preferred_element_type=jnp.float32
    ).astype(jnp.bfloat16)
    from_other = lax.ppermute(for_other, "dp", swap)
    grad_mine = scale[:, :1] * diff[:, :classes_here]
    bias_part = jnp.sum(grad_mine, axis=0)
    grad_head_weight = (
        lax.dot_general(
            act_plane, grad_mine.astype(jnp.bfloat16), rows, preferred_element_type=jnp.float32
        )
        + from_other.astype(jnp.float32)
    ).astype(jnp.bfloat16)[None]

    note = jnp.concatenate([log_joint, bias_other_part[None]], axis=1)
    pieces, grad_head_weight, note, bias_part = lax.optimization_barrier(
        (pieces, grad_head_weight, note, bias_part[None])
    )
    pairs = [[2 * chip, 2 * chip + 1] for chip in range(chips)]
    sums = lax.all_gather(sum_tails(pieces, note), "dp", axis_index_groups=pairs)
    grad_pooled, grad_gain, grad_shift, grad_head_bias, joint_mean = close_images(
        position, pieces, scale, normed, inverse, norm_gain, norm_bias, sums, bias_part
    )
    mean_loss = math.log(members) - joint_mean[0, 0]
    return (
        mean_loss,
        grad_pooled[None],
        grad_gain,
        grad_shift,
        grad_head_weight,
        grad_head_bias,
    )


def solution(mesh):
    in_specs = (
        P("member", "dp", None, None),
        P(),
        P("member", None),
        P("member", None),
        P("member", None, "dp"),
        P("member", "dp"),
    )
    out_specs = (
        P(),
        P("member", "dp", None),
        P("member", None),
        P("member", None),
        P("member", None, "dp"),
        P("member", "dp"),
    )
    return jax.shard_map(
        per_device, mesh=mesh, in_specs=in_specs, out_specs=out_specs, check_vma=False
    )
```

```python
import functools
import math

import jax
import jax.numpy as jnp
from jax import lax
from jax.experimental import pallas as pl
from jax.experimental.pallas import tpu as pltpu
from jax.sharding import PartitionSpec as P

norm_eps = 1e-06
loss_scale = 16.0


def norm_kernel(positions, total_ref, gain_ref, shift_ref, normed_ref, inverse_ref, act_ref):
    pooled = total_ref[...] / positions
    center = pooled - jnp.mean(pooled, axis=-1, keepdims=True)
    inverse = lax.rsqrt(jnp.mean(center * center, axis=-1, keepdims=True) + norm_eps)
    normed = center * inverse
    normed_ref[...] = normed
    inverse_ref[...] = jnp.broadcast_to(inverse, inverse_ref.shape)
    act = (normed * gain_ref[...] + shift_ref[...]).astype(jnp.bfloat16)
    act_ref[...] = jnp.broadcast_to(act[None], act_ref.shape)


def norm_copies(total, positions, gain_row, shift_row, copies):
    images, channels = total.shape
    whole = lambda *shape: pl.BlockSpec(shape, lambda i: (0,) * len(shape))
    return pl.pallas_call(
        functools.partial(norm_kernel, positions),
        grid=(1,),
        in_specs=[whole(images, channels), whole(1, channels), whole(1, channels)],
        out_specs=[
            whole(images, channels),
            whole(images, 128),
            whole(copies, images, channels),
        ],
        out_shape=[
            jax.ShapeDtypeStruct((images, channels), jnp.float32),
            jax.ShapeDtypeStruct((images, 128), jnp.float32),
            jax.ShapeDtypeStruct((copies, images, channels), jnp.bfloat16),
        ],
        compiler_params=pltpu.CompilerParams(vmem_limit_bytes=16 * 2**20),
    )(total, gain_row, shift_row)


def join_kernel(logp_ref, own_ref, partial_ref, act_ref, _, scale_ref, joint_ref, tail_ref):
    logp = logp_ref[...]
    top = jnp.max(logp, axis=0, keepdims=True)
    joint = top + jnp.log(jnp.sum(jnp.exp(logp - top), axis=0, keepdims=True))
    joint_ref[...] = joint
    scale = loss_scale * jnp.exp(own_ref[...] - joint)
    images = scale.shape[1]
    column = jnp.transpose(jnp.broadcast_to(scale, (128, images)))
    scale_ref[...] = column
    scaled = partial_ref[...] * column[:, :1]
    sums = [
        jnp.sum(scaled, axis=0, keepdims=True),
        jnp.sum(scaled * act_ref[...].astype(jnp.float32), axis=0, keepdims=True),
    ]
    high = [x.astype(jnp.bfloat16).astype(jnp.float32) for x in sums]
    low = [x - h for x, h in zip(sums, high)]
    width = tail_ref.shape[2]
    lines = [x[:, k : k + width] for x in high + low for k in range(0, x.shape[1], width)]
    tail = jnp.concatenate(lines, axis=0).astype(jnp.bfloat16)
    tail_ref[...] = jnp.broadcast_to(tail[None], tail_ref.shape)


def join_members(logp_all, label_logp, partial, act, chunks):
    images, channels = act.shape
    width = chunks.shape[2] - channels
    whole = lambda *shape: pl.BlockSpec(shape, lambda i: (0,) * len(shape))
    return pl.pallas_call(
        join_kernel,
        grid=(1,),
        in_specs=[
            whole(*logp_all.shape),
            whole(1, images),
            whole(images, channels),
            whole(images, channels),
            pl.BlockSpec(memory_space=pl.ANY),
        ],
        out_specs=[
            whole(images, 128),
            whole(1, images),
            pl.BlockSpec(chunks.shape[:2] + (width,), lambda i: (0, 0, channels // width)),
        ],
        out_shape=[
            jax.ShapeDtypeStruct((images, 128), jnp.float32),
            jax.ShapeDtypeStruct((1, images), jnp.float32),
            jax.ShapeDtypeStruct(chunks.shape, chunks.dtype),
        ],
        input_output_aliases={4: 2},
        compiler_params=pltpu.CompilerParams(vmem_limit_bytes=24 * 2**20),
    )(logp_all, label_logp, partial, act, chunks)


def close_kernel(
    _, pieces_ref, scale_ref, normed_ref, inverse_ref, gain_ref, shift_ref, sums_ref, *outs
):
    grad_ref, grad_gain_ref, grad_shift_ref = outs
    received = pieces_ref[0].astype(jnp.float32)
    for k in range(1, pieces_ref.shape[0]):
        received = received + pieces_ref[k].astype(jnp.float32)
    normed = normed_ref[...]
    gain = gain_ref[...]
    scaled = scale_ref[:, :1] * received * gain
    grad_ref[...] = inverse_ref[:, :1] * (
        scaled
        - jnp.mean(scaled, axis=-1, keepdims=True)
        - normed * jnp.mean(scaled * normed, axis=-1, keepdims=True)
    )
    sums = sums_ref[0] + sums_ref[1]
    grad_shift_ref[...] = sums[:1]
    grad_gain_ref[...] = (sums[1:] - shift_ref[...] * sums[:1]) / gain


def close_images(chip, pieces, scale, normed, inverse, gain_row, shift_row, sums):
    images, channels = normed.shape
    whole = lambda *shape: pl.BlockSpec(shape, lambda i, chip: (0,) * len(shape))
    return pl.pallas_call(
        close_kernel,
        grid_spec=pltpu.PrefetchScalarGridSpec(
            num_scalar_prefetch=1,
            grid=(1,),
            in_specs=[
                whole(pieces.shape[0], images, channels),
                pl.BlockSpec((images, 128), lambda i, chip: (chip[0], 0)),
                whole(images, channels),
                whole(images, 128),
                whole(1, channels),
                whole(1, channels),
                whole(*sums.shape),
            ],
            out_specs=[whole(images, channels), whole(1, channels), whole(1, channels)],
        ),
        out_shape=[
            jax.ShapeDtypeStruct((images, channels), jnp.float32),
            jax.ShapeDtypeStruct((1, channels), jnp.float32),
            jax.ShapeDtypeStruct((1, channels), jnp.float32),
        ],
        compiler_params=pltpu.CompilerParams(vmem_limit_bytes=16 * 2**20),
    )(jnp.reshape(chip, (1,)), pieces, scale, normed, inverse, gain_row, shift_row, sums)


def sum_tails_kernel(tails_ref, sums_ref):
    tail = tails_ref[0].astype(jnp.float32)
    for k in range(1, tails_ref.shape[0]):
        tail = tail + tails_ref[k].astype(jnp.float32)
    lines, width = tail.shape
    half, quarter = lines // 2, lines // 4
    tail = tail[:half] + tail[half:]
    for r in range(2):
        for k in range(quarter):
            sums_ref[r : r + 1, k * width : (k + 1) * width] = tail[r * quarter + k][None]


def sum_tails(pieces, channels):
    copies, lines, whole_width = pieces.shape
    width = whole_width - channels
    return pl.pallas_call(
        sum_tails_kernel,
        grid=(1,),
        in_specs=[pl.BlockSpec((copies, lines, width), lambda i: (0, 0, channels // width))],
        out_specs=pl.BlockSpec((2, channels), lambda i: (0, 0)),
        out_shape=jax.ShapeDtypeStruct((2, channels), jnp.float32),
        compiler_params=pltpu.CompilerParams(vmem_limit_bytes=16 * 2**20),
    )(pieces)


def per_device(features, labels, norm_gain, norm_bias, head_weight, head_bias):
    dp = lax.axis_size("dp")
    members = lax.axis_size("member")
    chips = dp // 2
    position = lax.axis_index("dp")
    core = lax.rem(position, 2)
    swap = [(i, i ^ 1) for i in range(dp)]
    planes = [[2 * chip + c for chip in range(chips)] for c in range(2)]

    def over_plane(x):
        return lax.all_to_all(x, "dp", 0, 0, axis_index_groups=planes)

    weight = head_weight[0]
    classes_here = weight.shape[1]
    gain_row = norm_gain[0]
    shift_row = norm_bias[0]
    images_here = features.shape[1]
    plane_images = chips * images_here

    weight_other = lax.ppermute(weight, "dp", swap)
    bias_other = lax.ppermute(head_bias[0], "dp", swap)

    normed, inverse, act_copies = norm_copies(
        jnp.sum(features[0], axis=1, dtype=jnp.float32),
        features.shape[2],
        norm_gain,
        norm_bias,
        chips,
    )
    channels = normed.shape[1]
    act_plane = over_plane(act_copies).reshape(plane_images, channels)

    plane_labels = lax.dynamic_index_in_dim(
        labels.reshape(chips, 2, images_here), core, axis=1, keepdims=False
    ).reshape(plane_images)
    class_ids = jnp.arange(classes_here, dtype=jnp.int32)
    both_ids = jnp.concatenate(
        [position * classes_here + class_ids, (position ^ 1) * classes_here + class_ids]
    )
    weight_both = jnp.concatenate([weight, weight_other], axis=1)
    bias_both = jnp.concatenate([head_bias[0], bias_other])
    onehot = plane_labels[:, None] == both_ids[None, :]
    logits = jnp.dot(act_plane, weight_both, preferred_element_type=jnp.float32) + bias_both
    top = jnp.max(logits, axis=1)
    total = jnp.sum(jnp.exp(logits - top[:, None]), axis=1)
    label_part = jnp.sum(jnp.where(onehot, logits, 0.0), axis=1)
    stats = jnp.stack([top + jnp.log(total), label_part])
    stats_all = over_plane(jnp.broadcast_to(stats[None], (chips,) + stats.shape))
    logs = stats_all[:, 0]
    logs_top = jnp.max(logs, axis=0)
    log_total = logs_top + jnp.log(jnp.sum(jnp.exp(logs - logs_top), axis=0))
    label_logp = jnp.sum(stats_all[:, 1], axis=0) - log_total

    logp_all = lax.all_to_all(
        jnp.broadcast_to(label_logp[None], (members, plane_images)), "member", 0, 0
    )

    diff = jnp.exp(logits - log_total[:, None]) - onehot.astype(jnp.float32)
    low = diff.astype(jnp.bfloat16)
    partial = lax.dot_general(
        low, weight_both, (((1,), (1,)), ((), ())), preferred_element_type=jnp.float32
    )
    tail_columns = 4 * channels // images_here
    chunks = jnp.pad(
        partial.astype(jnp.bfloat16).reshape(chips, images_here, channels),
        ((0, 0), (0, 0), (0, tail_columns)),
    )
    diff, partial, chunks = lax.optimization_barrier((diff, partial, chunks))
    scale, log_joint, chunks = join_members(
        logp_all, label_logp[None], partial, act_plane, chunks
    )
    pieces = over_plane(chunks)

    rows = (((0,), (0,)), ((), ()))
    grad_other = scale[:, :1] * diff[:, classes_here:]
    bias_other_part = jnp.sum(grad_other, axis=0)
    for_other = lax.dot_general(
        act_plane, grad_other.astype(jnp.bfloat16), rows, preferred_element_type=jnp.float32
    ).astype(jnp.bfloat16)
    from_other = lax.ppermute(for_other, "dp", swap)
    grad_mine = scale[:, :1] * diff[:, :classes_here]
    bias_part = jnp.sum(grad_mine, axis=0)
    grad_head_weight = (
        lax.dot_general(
            act_plane, grad_mine.astype(jnp.bfloat16), rows, preferred_element_type=jnp.float32
        )
        + from_other.astype(jnp.float32)
    ).astype(jnp.bfloat16)[None]

    note = jnp.concatenate([log_joint[0], bias_other_part])
    note = lax.ppermute(note, "dp", swap)
    mean_loss = math.log(members) - jnp.sum(log_joint[0] + note[:plane_images]) / (
        2 * plane_images
    )
    grad_head_bias = (bias_part + note[plane_images:])[None]
    pieces, grad_head_weight, grad_head_bias, mean_loss = lax.optimization_barrier(
        (pieces, grad_head_weight, grad_head_bias, mean_loss)
    )
    pairs = [[2 * chip, 2 * chip + 1] for chip in range(chips)]
    sums = lax.all_gather(sum_tails(pieces, channels), "dp", axis_index_groups=pairs)
    grad_pooled, grad_gain, grad_shift = close_images(
        position // 2, pieces, scale, normed, inverse, norm_gain, norm_bias, sums
    )
    return (
        mean_loss,
        grad_pooled[None],
        grad_gain,
        grad_shift,
        grad_head_weight,
        grad_head_bias,
    )


def solution(mesh):
    in_specs = (
        P("member", "dp", None, None),
        P(),
        P("member", None),
        P("member", None),
        P("member", None, "dp"),
        P("member", "dp"),
    )
    out_specs = (
        P(),
        P("member", "dp", None),
        P("member", None),
        P("member", None),
        P("member", None, "dp"),
        P("member", "dp"),
    )
    return jax.shard_map(
        per_device, mesh=mesh, in_specs=in_specs, out_specs=out_specs, check_vma=False
    )
```

```python
import functools
import math

import jax
import jax.numpy as jnp
from jax import lax
from jax.experimental import pallas as pl
from jax.experimental.pallas import tpu as pltpu
from jax.sharding import PartitionSpec as P

norm_eps = 1e-06
loss_scale = 16.0


def norm_kernel(positions, total_ref, gain_ref, shift_ref, normed_ref, inverse_ref, act_ref):
    pooled = total_ref[...] / positions
    center = pooled - jnp.mean(pooled, axis=-1, keepdims=True)
    inverse = lax.rsqrt(jnp.mean(center * center, axis=-1, keepdims=True) + norm_eps)
    normed = center * inverse
    normed_ref[...] = normed
    inverse_ref[...] = jnp.broadcast_to(inverse, inverse_ref.shape)
    act = (normed * gain_ref[...] + shift_ref[...]).astype(jnp.bfloat16)
    act_ref[...] = jnp.broadcast_to(act[None], act_ref.shape)


def norm_copies(total, positions, gain_row, shift_row, copies):
    images, channels = total.shape
    whole = lambda *shape: pl.BlockSpec(shape, lambda i: (0,) * len(shape))
    return pl.pallas_call(
        functools.partial(norm_kernel, positions),
        grid=(1,),
        in_specs=[whole(images, channels), whole(1, channels), whole(1, channels)],
        out_specs=[
            whole(images, channels),
            whole(images, 128),
            whole(copies, images, channels),
        ],
        out_shape=[
            jax.ShapeDtypeStruct((images, channels), jnp.float32),
            jax.ShapeDtypeStruct((images, 128), jnp.float32),
            jax.ShapeDtypeStruct((copies, images, channels), jnp.bfloat16),
        ],
        compiler_params=pltpu.CompilerParams(vmem_limit_bytes=16 * 2**20),
    )(total, gain_row, shift_row)


def join_kernel(logp_ref, own_ref, partial_ref, act_ref, _, scale_ref, joint_ref, tail_ref):
    logp = logp_ref[...]
    top = jnp.max(logp, axis=0, keepdims=True)
    joint = top + jnp.log(jnp.sum(jnp.exp(logp - top), axis=0, keepdims=True))
    joint_ref[...] = joint
    scale = loss_scale * jnp.exp(own_ref[...] - joint)
    images = scale.shape[1]
    column = jnp.transpose(jnp.broadcast_to(scale, (128, images)))
    scale_ref[...] = column
    scaled = partial_ref[...] * column[:, :1]
    sums = [
        jnp.sum(scaled, axis=0, keepdims=True),
        jnp.sum(scaled * act_ref[...].astype(jnp.float32), axis=0, keepdims=True),
    ]
    width = tail_ref.shape[2]
    lines = [x[:, k : k + width] for x in sums for k in range(0, x.shape[1], width)]
    tail = jnp.concatenate(lines, axis=0).astype(jnp.bfloat16)
    tail_ref[...] = jnp.broadcast_to(tail[None], tail_ref.shape)


def join_members(logp_all, label_logp, partial, act, chunks):
    images, channels = act.shape
    width = chunks.shape[2] - channels
    whole = lambda *shape: pl.BlockSpec(shape, lambda i: (0,) * len(shape))
    return pl.pallas_call(
        join_kernel,
        grid=(1,),
        in_specs=[
            whole(*logp_all.shape),
            whole(1, images),
            whole(images, channels),
            whole(images, channels),
            pl.BlockSpec(memory_space=pl.ANY),
        ],
        out_specs=[
            whole(images, 128),
            whole(1, images),
            pl.BlockSpec(chunks.shape[:2] + (width,), lambda i: (0, 0, channels // width)),
        ],
        out_shape=[
            jax.ShapeDtypeStruct((images, 128), jnp.float32),
            jax.ShapeDtypeStruct((1, images), jnp.float32),
            jax.ShapeDtypeStruct(chunks.shape, chunks.dtype),
        ],
        input_output_aliases={4: 2},
        compiler_params=pltpu.CompilerParams(vmem_limit_bytes=24 * 2**20),
    )(logp_all, label_logp, partial, act, chunks)


def close_kernel(
    _, pieces_ref, scale_ref, normed_ref, inverse_ref, gain_ref, shift_ref, sums_ref, *outs
):
    grad_ref, grad_gain_ref, grad_shift_ref = outs
    received = pieces_ref[0].astype(jnp.float32)
    for k in range(1, pieces_ref.shape[0]):
        received = received + pieces_ref[k].astype(jnp.float32)
    normed = normed_ref[...]
    gain = gain_ref[...]
    scaled = scale_ref[:, :1] * received * gain
    grad_ref[...] = inverse_ref[:, :1] * (
        scaled
        - jnp.mean(scaled, axis=-1, keepdims=True)
        - normed * jnp.mean(scaled * normed, axis=-1, keepdims=True)
    )
    sums = sums_ref[0] + sums_ref[1]
    grad_shift_ref[...] = sums[:1]
    grad_gain_ref[...] = (sums[1:] - shift_ref[...] * sums[:1]) / gain


def close_images(chip, pieces, scale, normed, inverse, gain_row, shift_row, sums):
    images, channels = normed.shape
    whole = lambda *shape: pl.BlockSpec(shape, lambda i, chip: (0,) * len(shape))
    return pl.pallas_call(
        close_kernel,
        grid_spec=pltpu.PrefetchScalarGridSpec(
            num_scalar_prefetch=1,
            grid=(1,),
            in_specs=[
                whole(pieces.shape[0], images, channels),
                pl.BlockSpec((images, 128), lambda i, chip: (chip[0], 0)),
                whole(images, channels),
                whole(images, 128),
                whole(1, channels),
                whole(1, channels),
                whole(*sums.shape),
            ],
            out_specs=[whole(images, channels), whole(1, channels), whole(1, channels)],
        ),
        out_shape=[
            jax.ShapeDtypeStruct((images, channels), jnp.float32),
            jax.ShapeDtypeStruct((1, channels), jnp.float32),
            jax.ShapeDtypeStruct((1, channels), jnp.float32),
        ],
        compiler_params=pltpu.CompilerParams(vmem_limit_bytes=16 * 2**20),
    )(jnp.reshape(chip, (1,)), pieces, scale, normed, inverse, gain_row, shift_row, sums)


def sum_tails_kernel(tails_ref, sums_ref):
    tail = tails_ref[0].astype(jnp.float32)
    for k in range(1, tails_ref.shape[0]):
        tail = tail + tails_ref[k].astype(jnp.float32)
    lines, width = tail.shape
    quarter = lines // 2
    for r in range(2):
        for k in range(quarter):
            sums_ref[r : r + 1, k * width : (k + 1) * width] = tail[r * quarter + k][None]


def sum_tails(pieces, channels):
    copies, lines, whole_width = pieces.shape
    width = whole_width - channels
    return pl.pallas_call(
        sum_tails_kernel,
        grid=(1,),
        in_specs=[pl.BlockSpec((copies, lines, width), lambda i: (0, 0, channels // width))],
        out_specs=pl.BlockSpec((2, channels), lambda i: (0, 0)),
        out_shape=jax.ShapeDtypeStruct((2, channels), jnp.float32),
        compiler_params=pltpu.CompilerParams(vmem_limit_bytes=16 * 2**20),
    )(pieces)


def per_device(features, labels, norm_gain, norm_bias, head_weight, head_bias):
    dp = lax.axis_size("dp")
    members = lax.axis_size("member")
    chips = dp // 2
    position = lax.axis_index("dp")
    core = lax.rem(position, 2)
    swap = [(i, i ^ 1) for i in range(dp)]
    planes = [[2 * chip + c for chip in range(chips)] for c in range(2)]

    def over_plane(x):
        return lax.all_to_all(x, "dp", 0, 0, axis_index_groups=planes)

    weight = head_weight[0]
    classes_here = weight.shape[1]
    gain_row = norm_gain[0]
    shift_row = norm_bias[0]
    images_here = features.shape[1]
    plane_images = chips * images_here

    weight_other = lax.ppermute(weight, "dp", swap)
    bias_other = lax.ppermute(head_bias[0], "dp", swap)

    normed, inverse, act_copies = norm_copies(
        jnp.sum(features[0], axis=1, dtype=jnp.float32),
        features.shape[2],
        norm_gain,
        norm_bias,
        chips,
    )
    channels = normed.shape[1]
    act_plane = over_plane(act_copies).reshape(plane_images, channels)

    plane_labels = lax.dynamic_index_in_dim(
        labels.reshape(chips, 2, images_here), core, axis=1, keepdims=False
    ).reshape(plane_images)
    class_ids = jnp.arange(classes_here, dtype=jnp.int32)
    both_ids = jnp.concatenate(
        [position * classes_here + class_ids, (position ^ 1) * classes_here + class_ids]
    )
    weight_both = jnp.concatenate([weight, weight_other], axis=1)
    bias_both = jnp.concatenate([head_bias[0], bias_other])
    onehot = plane_labels[:, None] == both_ids[None, :]
    logits = jnp.dot(act_plane, weight_both, preferred_element_type=jnp.float32) + bias_both
    top = jnp.max(logits, axis=1)
    total = jnp.sum(jnp.exp(logits - top[:, None]), axis=1)
    label_part = jnp.sum(jnp.where(onehot, logits, 0.0), axis=1)
    stats = jnp.stack([top + jnp.log(total), label_part])
    stats_all = over_plane(jnp.broadcast_to(stats[None], (chips,) + stats.shape))
    logs = stats_all[:, 0]
    logs_top = jnp.max(logs, axis=0)
    log_total = logs_top + jnp.log(jnp.sum(jnp.exp(logs - logs_top), axis=0))
    label_logp = jnp.sum(stats_all[:, 1], axis=0) - log_total

    logp_all = lax.all_to_all(
        jnp.broadcast_to(label_logp[None], (members, plane_images)), "member", 0, 0
    )

    diff = jnp.exp(logits - log_total[:, None]) - onehot.astype(jnp.float32)
    low = diff.astype(jnp.bfloat16)
    partial = lax.dot_general(
        low, weight_both, (((1,), (1,)), ((), ())), preferred_element_type=jnp.float32
    )
    tail_columns = 2 * channels // images_here
    chunks = jnp.pad(
        partial.astype(jnp.bfloat16).reshape(chips, images_here, channels),
        ((0, 0), (0, 0), (0, tail_columns)),
    )
    diff, partial, chunks = lax.optimization_barrier((diff, partial, chunks))
    scale, log_joint, chunks = join_members(
        logp_all, label_logp[None], partial, act_plane, chunks
    )
    pieces = over_plane(chunks)

    rows = (((0,), (0,)), ((), ()))
    grad_other = scale[:, :1] * diff[:, classes_here:]
    bias_other_part = jnp.sum(grad_other, axis=0)
    for_other = lax.dot_general(
        act_plane, grad_other.astype(jnp.bfloat16), rows, preferred_element_type=jnp.float32
    ).astype(jnp.bfloat16)
    from_other = lax.ppermute(for_other, "dp", swap)
    grad_mine = scale[:, :1] * diff[:, :classes_here]
    bias_part = jnp.sum(grad_mine, axis=0)
    grad_head_weight = (
        lax.dot_general(
            act_plane, grad_mine.astype(jnp.bfloat16), rows, preferred_element_type=jnp.float32
        )
        + from_other.astype(jnp.float32)
    ).astype(jnp.bfloat16)[None]

    note = jnp.concatenate([log_joint[0], bias_other_part])
    note = lax.ppermute(note, "dp", swap)
    mean_loss = math.log(members) - jnp.sum(log_joint[0] + note[:plane_images]) / (
        2 * plane_images
    )
    grad_head_bias = (bias_part + note[plane_images:])[None]
    pieces, grad_head_weight, grad_head_bias, mean_loss = lax.optimization_barrier(
        (pieces, grad_head_weight, grad_head_bias, mean_loss)
    )
    pairs = [[2 * chip, 2 * chip + 1] for chip in range(chips)]
    sums = lax.all_gather(sum_tails(pieces, channels), "dp", axis_index_groups=pairs)
    grad_pooled, grad_gain, grad_shift = close_images(
        position // 2, pieces, scale, normed, inverse, norm_gain, norm_bias, sums
    )
    return (
        mean_loss,
        grad_pooled[None],
        grad_gain,
        grad_shift,
        grad_head_weight,
        grad_head_bias,
    )


def solution(mesh):
    in_specs = (
        P("member", "dp", None, None),
        P(),
        P("member", None),
        P("member", None),
        P("member", None, "dp"),
        P("member", "dp"),
    )
    out_specs = (
        P(),
        P("member", "dp", None),
        P("member", None),
        P("member", None),
        P("member", None, "dp"),
        P("member", "dp"),
    )
    return jax.shard_map(
        per_device, mesh=mesh, in_specs=in_specs, out_specs=out_specs, check_vma=False
    )
```

```python
import functools
import math

import jax
import jax.numpy as jnp
from jax import lax
from jax.experimental import pallas as pl
from jax.experimental.pallas import tpu as pltpu
from jax.sharding import PartitionSpec as P

norm_eps = 1e-06
loss_scale = 16.0


def norm_kernel(positions, total_ref, gain_ref, shift_ref, normed_ref, inverse_ref, act_ref):
    pooled = total_ref[...] / positions
    center = pooled - jnp.mean(pooled, axis=-1, keepdims=True)
    inverse = lax.rsqrt(jnp.mean(center * center, axis=-1, keepdims=True) + norm_eps)
    normed = center * inverse
    normed_ref[...] = normed
    inverse_ref[...] = jnp.broadcast_to(inverse, inverse_ref.shape)
    act = (normed * gain_ref[...] + shift_ref[...]).astype(jnp.bfloat16)
    act_ref[...] = jnp.broadcast_to(act[None], act_ref.shape)


def norm_copies(total, positions, gain_row, shift_row, copies):
    images, channels = total.shape
    whole = lambda *shape: pl.BlockSpec(shape, lambda i: (0,) * len(shape))
    return pl.pallas_call(
        functools.partial(norm_kernel, positions),
        grid=(1,),
        in_specs=[whole(images, channels), whole(1, channels), whole(1, channels)],
        out_specs=[
            whole(images, channels),
            whole(images, 128),
            whole(copies, images, channels),
        ],
        out_shape=[
            jax.ShapeDtypeStruct((images, channels), jnp.float32),
            jax.ShapeDtypeStruct((images, 128), jnp.float32),
            jax.ShapeDtypeStruct((copies, images, channels), jnp.bfloat16),
        ],
        compiler_params=pltpu.CompilerParams(vmem_limit_bytes=16 * 2**20),
    )(total, gain_row, shift_row)


def join_kernel(logp_ref, own_ref, partial_ref, act_ref, _, scale_ref, joint_ref, tail_ref):
    logp = logp_ref[...]
    top = jnp.max(logp, axis=0, keepdims=True)
    joint = top + jnp.log(jnp.sum(jnp.exp(logp - top), axis=0, keepdims=True))
    joint_ref[...] = joint
    scale = loss_scale * jnp.exp(own_ref[...] - joint)
    images = scale.shape[1]
    column = jnp.transpose(jnp.broadcast_to(scale, (128, images)))
    scale_ref[...] = column
    scaled = partial_ref[...] * column[:, :1]
    sums = [
        jnp.sum(scaled, axis=0, keepdims=True),
        jnp.sum(scaled * act_ref[...].astype(jnp.float32), axis=0, keepdims=True),
    ]
    width = tail_ref.shape[2]
    lines = [x[:, k : k + width] for x in sums for k in range(0, x.shape[1], width)]
    tail = jnp.concatenate(lines, axis=0).astype(jnp.bfloat16)
    tail_ref[...] = jnp.broadcast_to(tail[None], tail_ref.shape)


def join_members(logp_all, label_logp, partial, act, chunks):
    images, channels = act.shape
    width = chunks.shape[2] - channels
    whole = lambda *shape: pl.BlockSpec(shape, lambda i: (0,) * len(shape))
    return pl.pallas_call(
        join_kernel,
        grid=(1,),
        in_specs=[
            whole(*logp_all.shape),
            whole(1, images),
            whole(images, channels),
            whole(images, channels),
            pl.BlockSpec(memory_space=pl.ANY),
        ],
        out_specs=[
            whole(images, 128),
            whole(1, images),
            pl.BlockSpec(chunks.shape[:2] + (width,), lambda i: (0, 0, channels // width)),
        ],
        out_shape=[
            jax.ShapeDtypeStruct((images, 128), jnp.float32),
            jax.ShapeDtypeStruct((1, images), jnp.float32),
            jax.ShapeDtypeStruct(chunks.shape, chunks.dtype),
        ],
        input_output_aliases={4: 2},
        compiler_params=pltpu.CompilerParams(vmem_limit_bytes=24 * 2**20),
    )(logp_all, label_logp, partial, act, chunks)


def close_kernel(
    _, pieces_ref, scale_ref, normed_ref, inverse_ref, gain_ref, shift_ref, sums_ref, *outs
):
    grad_ref, grad_gain_ref, grad_shift_ref = outs
    received = pieces_ref[0].astype(jnp.float32)
    for k in range(1, pieces_ref.shape[0]):
        received = received + pieces_ref[k].astype(jnp.float32)
    normed = normed_ref[...]
    gain = gain_ref[...]
    scaled = scale_ref[:, :1] * received * gain
    grad_ref[...] = inverse_ref[:, :1] * (
        scaled
        - jnp.mean(scaled, axis=-1, keepdims=True)
        - normed * jnp.mean(scaled * normed, axis=-1, keepdims=True)
    )
    sums = sums_ref[0] + sums_ref[1]
    grad_shift_ref[...] = sums[:1]
    grad_gain_ref[...] = (sums[1:] - shift_ref[...] * sums[:1]) / gain


def close_images(chip, pieces, scale, normed, inverse, gain_row, shift_row, sums):
    images, channels = normed.shape
    whole = lambda *shape: pl.BlockSpec(shape, lambda i, chip: (0,) * len(shape))
    return pl.pallas_call(
        close_kernel,
        grid_spec=pltpu.PrefetchScalarGridSpec(
            num_scalar_prefetch=1,
            grid=(1,),
            in_specs=[
                whole(pieces.shape[0], images, channels),
                pl.BlockSpec((images, 128), lambda i, chip: (chip[0], 0)),
                whole(images, channels),
                whole(images, 128),
                whole(1, channels),
                whole(1, channels),
                whole(*sums.shape),
            ],
            out_specs=[whole(images, channels), whole(1, channels), whole(1, channels)],
        ),
        out_shape=[
            jax.ShapeDtypeStruct((images, channels), jnp.float32),
            jax.ShapeDtypeStruct((1, channels), jnp.float32),
            jax.ShapeDtypeStruct((1, channels), jnp.float32),
        ],
        compiler_params=pltpu.CompilerParams(vmem_limit_bytes=16 * 2**20),
    )(jnp.reshape(chip, (1,)), pieces, scale, normed, inverse, gain_row, shift_row, sums)


def sum_tails_kernel(tails_ref, sums_ref):
    tail = tails_ref[0].astype(jnp.float32)
    for k in range(1, tails_ref.shape[0]):
        tail = tail + tails_ref[k].astype(jnp.float32)
    lines, width = tail.shape
    quarter = lines // 2
    for r in range(2):
        for k in range(quarter):
            sums_ref[r : r + 1, k * width : (k + 1) * width] = tail[r * quarter + k][None]


def sum_tails(pieces, channels):
    copies, lines, whole_width = pieces.shape
    width = whole_width - channels
    return pl.pallas_call(
        sum_tails_kernel,
        grid=(1,),
        in_specs=[pl.BlockSpec((copies, lines, width), lambda i: (0, 0, channels // width))],
        out_specs=pl.BlockSpec((2, channels), lambda i: (0, 0)),
        out_shape=jax.ShapeDtypeStruct((2, channels), jnp.float32),
        compiler_params=pltpu.CompilerParams(vmem_limit_bytes=16 * 2**20),
    )(pieces)


def per_device(features, labels, norm_gain, norm_bias, head_weight, head_bias):
    dp = lax.axis_size("dp")
    members = lax.axis_size("member")
    chips = dp // 2
    position = lax.axis_index("dp")
    core = lax.rem(position, 2)
    swap = [(i, i ^ 1) for i in range(dp)]
    planes = [
        [2 * chip for chip in range(chips)],
        [2 * chip + 1 for chip in reversed(range(chips))],
    ]
    slot = jnp.where(core == 0, position // 2, chips - 1 - position // 2)

    def over_plane(x):
        return lax.all_to_all(x, "dp", 0, 0, axis_index_groups=planes)

    weight = head_weight[0]
    classes_here = weight.shape[1]
    gain_row = norm_gain[0]
    shift_row = norm_bias[0]
    images_here = features.shape[1]
    plane_images = chips * images_here

    weight_other = lax.ppermute(weight, "dp", swap)
    bias_other = lax.ppermute(head_bias[0], "dp", swap)

    normed, inverse, act_copies = norm_copies(
        jnp.sum(features[0], axis=1, dtype=jnp.float32),
        features.shape[2],
        norm_gain,
        norm_bias,
        chips,
    )
    channels = normed.shape[1]
    act_plane = over_plane(act_copies).reshape(plane_images, channels)

    by_chip = labels.reshape(chips, 2, images_here)
    plane_labels = jnp.where(core == 0, by_chip[:, 0], by_chip[::-1, 1]).reshape(plane_images)
    class_ids = jnp.arange(classes_here, dtype=jnp.int32)
    both_ids = jnp.concatenate(
        [position * classes_here + class_ids, (position ^ 1) * classes_here + class_ids]
    )
    weight_both = jnp.concatenate([weight, weight_other], axis=1)
    bias_both = jnp.concatenate([head_bias[0], bias_other])
    onehot = plane_labels[:, None] == both_ids[None, :]
    logits = jnp.dot(act_plane, weight_both, preferred_element_type=jnp.float32) + bias_both
    top = jnp.max(logits, axis=1)
    total = jnp.sum(jnp.exp(logits - top[:, None]), axis=1)
    label_part = jnp.sum(jnp.where(onehot, logits, 0.0), axis=1)
    stats = jnp.stack([top + jnp.log(total), label_part])
    stats_all = over_plane(jnp.broadcast_to(stats[None], (chips,) + stats.shape))
    logs = stats_all[:, 0]
    logs_top = jnp.max(logs, axis=0)
    log_total = logs_top + jnp.log(jnp.sum(jnp.exp(logs - logs_top), axis=0))
    label_logp = jnp.sum(stats_all[:, 1], axis=0) - log_total

    logp_all = lax.all_to_all(
        jnp.broadcast_to(label_logp[None], (members, plane_images)), "member", 0, 0
    )

    diff = jnp.exp(logits - log_total[:, None]) - onehot.astype(jnp.float32)
    low = diff.astype(jnp.bfloat16)
    partial = lax.dot_general(
        low, weight_both, (((1,), (1,)), ((), ())), preferred_element_type=jnp.float32
    )
    tail_columns = 2 * channels // images_here
    chunks = jnp.pad(
        partial.astype(jnp.bfloat16).reshape(chips, images_here, channels),
        ((0, 0), (0, 0), (0, tail_columns)),
    )
    diff, partial, chunks = lax.optimization_barrier((diff, partial, chunks))
    scale, log_joint, chunks = join_members(
        logp_all, label_logp[None], partial, act_plane, chunks
    )
    pieces = over_plane(chunks)

    rows = (((0,), (0,)), ((), ()))
    grad_other = scale[:, :1] * diff[:, classes_here:]
    bias_other_part = jnp.sum(grad_other, axis=0)
    for_other = lax.dot_general(
        act_plane, grad_other.astype(jnp.bfloat16), rows, preferred_element_type=jnp.float32
    ).astype(jnp.bfloat16)
    from_other = lax.ppermute(for_other, "dp", swap)
    grad_mine = scale[:, :1] * diff[:, :classes_here]
    bias_part = jnp.sum(grad_mine, axis=0)
    grad_head_weight = (
        lax.dot_general(
            act_plane, grad_mine.astype(jnp.bfloat16), rows, preferred_element_type=jnp.float32
        )
        + from_other.astype(jnp.float32)
    ).astype(jnp.bfloat16)[None]

    note = jnp.concatenate([log_joint[0], bias_other_part])
    note = lax.ppermute(note, "dp", swap)
    mean_loss = math.log(members) - jnp.sum(log_joint[0] + note[:plane_images]) / (
        2 * plane_images
    )
    grad_head_bias = (bias_part + note[plane_images:])[None]
    pieces, grad_head_weight, grad_head_bias, mean_loss = lax.optimization_barrier(
        (pieces, grad_head_weight, grad_head_bias, mean_loss)
    )
    pairs = [[2 * chip, 2 * chip + 1] for chip in range(chips)]
    sums = lax.all_gather(sum_tails(pieces, channels), "dp", axis_index_groups=pairs)
    grad_pooled, grad_gain, grad_shift = close_images(
        slot, pieces, scale, normed, inverse, norm_gain, norm_bias, sums
    )
    return (
        mean_loss,
        grad_pooled[None],
        grad_gain,
        grad_shift,
        grad_head_weight,
        grad_head_bias,
    )


def solution(mesh):
    in_specs = (
        P("member", "dp", None, None),
        P(),
        P("member", None),
        P("member", None),
        P("member", None, "dp"),
        P("member", "dp"),
    )
    out_specs = (
        P(),
        P("member", "dp", None),
        P("member", None),
        P("member", None),
        P("member", None, "dp"),
        P("member", "dp"),
    )
    return jax.shard_map(
        per_device, mesh=mesh, in_specs=in_specs, out_specs=out_specs, check_vma=False
    )
```

```python
import functools
import math

import jax
import jax.numpy as jnp
from jax import lax
from jax.experimental import pallas as pl
from jax.experimental.pallas import tpu as pltpu
from jax.sharding import PartitionSpec as P

norm_eps = 1e-06
loss_scale = 16.0


def norm_kernel(positions, total_ref, gain_ref, shift_ref, normed_ref, inverse_ref, act_ref):
    pooled = total_ref[...] / positions
    center = pooled - jnp.mean(pooled, axis=-1, keepdims=True)
    inverse = lax.rsqrt(jnp.mean(center * center, axis=-1, keepdims=True) + norm_eps)
    normed = center * inverse
    normed_ref[...] = normed
    inverse_ref[...] = jnp.broadcast_to(inverse, inverse_ref.shape)
    act = (normed * gain_ref[...] + shift_ref[...]).astype(jnp.bfloat16)
    act_ref[...] = jnp.broadcast_to(act[None], act_ref.shape)


def norm_copies(total, positions, gain_row, shift_row, copies):
    images, channels = total.shape
    whole = lambda *shape: pl.BlockSpec(shape, lambda i: (0,) * len(shape))
    return pl.pallas_call(
        functools.partial(norm_kernel, positions),
        grid=(1,),
        in_specs=[whole(images, channels), whole(1, channels), whole(1, channels)],
        out_specs=[
            whole(images, channels),
            whole(images, 128),
            whole(copies, images, channels),
        ],
        out_shape=[
            jax.ShapeDtypeStruct((images, channels), jnp.float32),
            jax.ShapeDtypeStruct((images, 128), jnp.float32),
            jax.ShapeDtypeStruct((copies, images, channels), jnp.bfloat16),
        ],
        compiler_params=pltpu.CompilerParams(vmem_limit_bytes=16 * 2**20),
    )(total, gain_row, shift_row)


def join_kernel(logp_ref, own_ref, partial_ref, act_ref, _, scale_ref, joint_ref, tail_ref):
    logp = logp_ref[...]
    top = jnp.max(logp, axis=0, keepdims=True)
    joint = top + jnp.log(jnp.sum(jnp.exp(logp - top), axis=0, keepdims=True))
    joint_ref[...] = joint
    scale = loss_scale * jnp.exp(own_ref[...] - joint)
    images = scale.shape[1]
    column = jnp.transpose(jnp.broadcast_to(scale, (128, images)))
    scale_ref[...] = column
    scaled = partial_ref[...] * column[:, :1]
    sums = [
        jnp.sum(scaled, axis=0, keepdims=True),
        jnp.sum(scaled * act_ref[...].astype(jnp.float32), axis=0, keepdims=True),
    ]
    width = tail_ref.shape[2]
    lines = [x[:, k : k + width] for x in sums for k in range(0, x.shape[1], width)]
    tail = jnp.concatenate(lines, axis=0).astype(jnp.bfloat16)
    tail_ref[...] = jnp.broadcast_to(tail[None], tail_ref.shape)


def join_members(logp_all, label_logp, partial, act, chunks):
    images, channels = act.shape
    width = chunks.shape[2] - channels
    whole = lambda *shape: pl.BlockSpec(shape, lambda i: (0,) * len(shape))
    return pl.pallas_call(
        join_kernel,
        grid=(1,),
        in_specs=[
            whole(*logp_all.shape),
            whole(1, images),
            whole(images, channels),
            whole(images, channels),
            pl.BlockSpec(memory_space=pl.ANY),
        ],
        out_specs=[
            whole(images, 128),
            whole(1, images),
            pl.BlockSpec(chunks.shape[:2] + (width,), lambda i: (0, 0, channels // width)),
        ],
        out_shape=[
            jax.ShapeDtypeStruct((images, 128), jnp.float32),
            jax.ShapeDtypeStruct((1, images), jnp.float32),
            jax.ShapeDtypeStruct(chunks.shape, chunks.dtype),
        ],
        input_output_aliases={4: 2},
        compiler_params=pltpu.CompilerParams(vmem_limit_bytes=24 * 2**20),
    )(logp_all, label_logp, partial, act, chunks)


def close_kernel(
    _, pieces_ref, scale_ref, normed_ref, inverse_ref, gain_ref, shift_ref, sums_ref, *outs
):
    grad_ref, grad_gain_ref, grad_shift_ref = outs
    received = pieces_ref[0].astype(jnp.float32)
    for k in range(1, pieces_ref.shape[0]):
        received = received + pieces_ref[k].astype(jnp.float32)
    normed = normed_ref[...]
    gain = gain_ref[...]
    scaled = scale_ref[:, :1] * received * gain
    grad_ref[...] = inverse_ref[:, :1] * (
        scaled
        - jnp.mean(scaled, axis=-1, keepdims=True)
        - normed * jnp.mean(scaled * normed, axis=-1, keepdims=True)
    )
    sums = sums_ref[0] + sums_ref[1]
    grad_shift_ref[...] = sums[:1]
    grad_gain_ref[...] = (sums[1:] - shift_ref[...] * sums[:1]) / gain


def close_images(chip, pieces, scale, normed, inverse, gain_row, shift_row, sums):
    images, channels = normed.shape
    whole = lambda *shape: pl.BlockSpec(shape, lambda i, chip: (0,) * len(shape))
    return pl.pallas_call(
        close_kernel,
        grid_spec=pltpu.PrefetchScalarGridSpec(
            num_scalar_prefetch=1,
            grid=(1,),
            in_specs=[
                whole(pieces.shape[0], images, channels),
                pl.BlockSpec((images, 128), lambda i, chip: (chip[0], 0)),
                whole(images, channels),
                whole(images, 128),
                whole(1, channels),
                whole(1, channels),
                whole(*sums.shape),
            ],
            out_specs=[whole(images, channels), whole(1, channels), whole(1, channels)],
        ),
        out_shape=[
            jax.ShapeDtypeStruct((images, channels), jnp.float32),
            jax.ShapeDtypeStruct((1, channels), jnp.float32),
            jax.ShapeDtypeStruct((1, channels), jnp.float32),
        ],
        compiler_params=pltpu.CompilerParams(vmem_limit_bytes=16 * 2**20),
    )(jnp.reshape(chip, (1,)), pieces, scale, normed, inverse, gain_row, shift_row, sums)


def sum_tails_kernel(tails_ref, sums_ref):
    tail = tails_ref[0].astype(jnp.float32)
    for k in range(1, tails_ref.shape[0]):
        tail = tail + tails_ref[k].astype(jnp.float32)
    lines, width = tail.shape
    quarter = lines // 2
    for r in range(2):
        for k in range(quarter):
            sums_ref[r : r + 1, k * width : (k + 1) * width] = tail[r * quarter + k][None]


def sum_tails(pieces, channels):
    copies, lines, whole_width = pieces.shape
    width = whole_width - channels
    return pl.pallas_call(
        sum_tails_kernel,
        grid=(1,),
        in_specs=[pl.BlockSpec((copies, lines, width), lambda i: (0, 0, channels // width))],
        out_specs=pl.BlockSpec((2, channels), lambda i: (0, 0)),
        out_shape=jax.ShapeDtypeStruct((2, channels), jnp.float32),
        compiler_params=pltpu.CompilerParams(vmem_limit_bytes=16 * 2**20),
    )(pieces)


def per_device(features, labels, norm_gain, norm_bias, head_weight, head_bias):
    dp = lax.axis_size("dp")
    members = lax.axis_size("member")
    chips = dp // 2
    position = lax.axis_index("dp")
    core = lax.rem(position, 2)
    swap = [(i, i ^ 1) for i in range(dp)]
    order = [(7 * k) % chips for k in range(chips)]
    planes = [[2 * chip for chip in order], [2 * chip + 1 for chip in reversed(order)]]
    forth = jnp.sum(jnp.where(jnp.array(order) == position // 2, jnp.arange(chips), 0))
    slot = jnp.where(core == 0, forth, chips - 1 - forth).astype(jnp.int32)

    def over_plane(x):
        return lax.all_to_all(x, "dp", 0, 0, axis_index_groups=planes)

    weight = head_weight[0]
    classes_here = weight.shape[1]
    gain_row = norm_gain[0]
    shift_row = norm_bias[0]
    images_here = features.shape[1]
    plane_images = chips * images_here

    weight_other = lax.ppermute(weight, "dp", swap)
    bias_other = lax.ppermute(head_bias[0], "dp", swap)

    normed, inverse, act_copies = norm_copies(
        jnp.sum(features[0], axis=1, dtype=jnp.float32),
        features.shape[2],
        norm_gain,
        norm_bias,
        chips,
    )
    channels = normed.shape[1]
    act_plane = over_plane(act_copies).reshape(plane_images, channels)

    by_chip = labels.reshape(chips, 2, images_here)
    plane_labels = jnp.where(
        core == 0,
        jnp.concatenate([by_chip[chip, 0] for chip in order]),
        jnp.concatenate([by_chip[chip, 1] for chip in reversed(order)]),
    )
    class_ids = jnp.arange(classes_here, dtype=jnp.int32)
    both_ids = jnp.concatenate(
        [position * classes_here + class_ids, (position ^ 1) * classes_here + class_ids]
    )
    weight_both = jnp.concatenate([weight, weight_other], axis=1)
    bias_both = jnp.concatenate([head_bias[0], bias_other])
    onehot = plane_labels[:, None] == both_ids[None, :]
    logits = jnp.dot(act_plane, weight_both, preferred_element_type=jnp.float32) + bias_both
    top = jnp.max(logits, axis=1)
    total = jnp.sum(jnp.exp(logits - top[:, None]), axis=1)
    label_part = jnp.sum(jnp.where(onehot, logits, 0.0), axis=1)
    stats = jnp.stack([top + jnp.log(total), label_part])
    stats_all = over_plane(jnp.broadcast_to(stats[None], (chips,) + stats.shape))
    logs = stats_all[:, 0]
    logs_top = jnp.max(logs, axis=0)
    log_total = logs_top + jnp.log(jnp.sum(jnp.exp(logs - logs_top), axis=0))
    label_logp = jnp.sum(stats_all[:, 1], axis=0) - log_total

    logp_all = lax.all_to_all(
        jnp.broadcast_to(label_logp[None], (members, plane_images)), "member", 0, 0
    )

    diff = jnp.exp(logits - log_total[:, None]) - onehot.astype(jnp.float32)
    low = diff.astype(jnp.bfloat16)
    partial = lax.dot_general(
        low, weight_both, (((1,), (1,)), ((), ())), preferred_element_type=jnp.float32
    )
    tail_columns = 2 * channels // images_here
    chunks = jnp.pad(
        partial.astype(jnp.bfloat16).reshape(chips, images_here, channels),
        ((0, 0), (0, 0), (0, tail_columns)),
    )
    diff, partial, chunks = lax.optimization_barrier((diff, partial, chunks))
    scale, log_joint, chunks = join_members(
        logp_all, label_logp[None], partial, act_plane, chunks
    )
    pieces = over_plane(chunks)

    rows = (((0,), (0,)), ((), ()))
    grad_other = scale[:, :1] * diff[:, classes_here:]
    bias_other_part = jnp.sum(grad_other, axis=0)
    for_other = lax.dot_general(
        act_plane, grad_other.astype(jnp.bfloat16), rows, preferred_element_type=jnp.float32
    ).astype(jnp.bfloat16)
    from_other = lax.ppermute(for_other, "dp", swap)
    grad_mine = scale[:, :1] * diff[:, :classes_here]
    bias_part = jnp.sum(grad_mine, axis=0)
    grad_head_weight = (
        lax.dot_general(
            act_plane, grad_mine.astype(jnp.bfloat16), rows, preferred_element_type=jnp.float32
        )
        + from_other.astype(jnp.float32)
    ).astype(jnp.bfloat16)[None]

    note = jnp.concatenate([log_joint[0], bias_other_part])
    note = lax.ppermute(note, "dp", swap)
    mean_loss = math.log(members) - jnp.sum(log_joint[0] + note[:plane_images]) / (
        2 * plane_images
    )
    grad_head_bias = (bias_part + note[plane_images:])[None]
    pieces, grad_head_weight, grad_head_bias, mean_loss = lax.optimization_barrier(
        (pieces, grad_head_weight, grad_head_bias, mean_loss)
    )
    pairs = [[2 * chip, 2 * chip + 1] for chip in range(chips)]
    sums = lax.all_gather(sum_tails(pieces, channels), "dp", axis_index_groups=pairs)
    grad_pooled, grad_gain, grad_shift = close_images(
        slot, pieces, scale, normed, inverse, norm_gain, norm_bias, sums
    )
    return (
        mean_loss,
        grad_pooled[None],
        grad_gain,
        grad_shift,
        grad_head_weight,
        grad_head_bias,
    )


def solution(mesh):
    in_specs = (
        P("member", "dp", None, None),
        P(),
        P("member", None),
        P("member", None),
        P("member", None, "dp"),
        P("member", "dp"),
    )
    out_specs = (
        P(),
        P("member", "dp", None),
        P("member", None),
        P("member", None),
        P("member", None, "dp"),
        P("member", "dp"),
    )
    return jax.shard_map(
        per_device, mesh=mesh, in_specs=in_specs, out_specs=out_specs, check_vma=False
    )
```
